256 devices in a mesh: seq: 16 (over z, core), chan: 16 (over x, y).
Axes of the slice: x: 4, y: 4, z: 8, core: 2. Of those that a mesh axis runs over, the one named last changes fastest.
Arguments:
- grad_out: bfloat16 [8192, 8192], P('seq', 'chan'), may hold values from -6 to 6
- qkv_saved: bfloat16 [8192, 3, 8192], P('seq', None, 'chan'), may hold values from -6 to 6
- conv_saved: bfloat16 [8192, 8192], P('seq', 'chan'), may hold values from -6 to 6
- long_taps: bfloat16 [8192, 512], P('seq', 'chan'), may hold values from -1 to 1
- short_taps: float32 [3, 3, 8192], P(None, None, 'chan'), may hold values from -3 to 3
Outputs:
- grad_proj: bfloat16 [8192, 3, 8192], P(('seq', 'chan'))
The draws below stay inside these ranges and needn't reach their ends.
All inputs are finite; a program needn't handle non-finite values.
Results may differ from the reference program's by a relative error of at most 0.0042.
Values may be sent and summed in bfloat16 or wider, within the bound.
A program may use at most 64 MiB of HBM per device.

```python
import math
import jax
import jax.numpy as jnp
from jax import lax

D = 8192
GROUP = 16
SHORT = 3
TOKENS = 8192
GROUPS = 512


def draw_long_taps(key, part):
    key_tau, key_noise = jax.random.split(jax.random.fold_in(key, 7))
    lags = jnp.arange(TOKENS, dtype=jnp.float32)[:, None]
    log_tau = jax.random.uniform(key_tau, (1, GROUPS), jnp.float32, math.log(32.0), math.log(4 * TOKENS))
    noise = jnp.clip(jax.random.normal(key_noise, (TOKENS, GROUPS), jnp.float32), -4.0, 4.0)
    decay = jnp.exp(log_tau)
    spread = jnp.sqrt(2.0 / jnp.minimum(decay, float(TOKENS)))
    return (noise * spread * jnp.exp(-lags / decay)).astype(jnp.bfloat16)


def levels(own_key, extent, cuts, smallest, top_value):
    level = 1.0
    for dim, shards_of in cuts:
        heights = jax.random.uniform(jax.random.fold_in(jax.random.fold_in(own_key, 6), dim), (shards_of,), jnp.float32, smallest / len(cuts), top_value / len(cuts))
        level = level * jnp.repeat(jnp.exp(heights), extent[dim] // shards_of).reshape((-1,) + (1,) * (len(extent) - 1 - dim))
    return level


def centred(stream_key, dims, width, bound, cuts=(), kind=jnp.bfloat16):
    values = jax.random.normal(stream_key, dims, jnp.float32) * width
    if len(cuts) > 0:
        values = levels(stream_key, dims, cuts, -0.22, 0.18) * values
    return jnp.clip(values, min=-bound, max=bound).astype(kind)


def setup_inputs(seed: int = 0) -> dict:
    arg_keys = jax.random.split(jax.random.key(seed), 6)
    grad_out = centred(arg_keys[0], (TOKENS, D), 1.0, 6.0, ((0, 16), (1, 16)))
    qkv_saved = centred(arg_keys[1], (TOKENS, 3, D), 1.0, 6.0, ((0, 16), (2, 16)))
    conv_saved = centred(arg_keys[2], (TOKENS, D), 1.0, 6.0, ((0, 16), (1, 16)))
    long_taps = draw_long_taps(jax.random.fold_in(arg_keys[5], 71), 0)
    short_taps = centred(arg_keys[4], (3, SHORT, D), 0.6, 3.0, ((2, 16),), jnp.float32)
    return {"grad_out": grad_out, "qkv_saved": qkv_saved, "conv_saved": conv_saved, "long_taps": long_taps, "short_taps": short_taps}


def correlate_block(pair):
    grads, filters = pair
    length = grads.shape[0]
    reverse = grads[::-1]
    spectrum = jnp.fft.rfft(filters, 2 * length, axis=0) * jnp.fft.rfft(reverse, 2 * length, axis=0)
    return jnp.fft.irfft(spectrum, 2 * length, axis=0)[:length][::-1]


def reference(grad_out, qkv_saved, conv_saved, long_taps, short_taps):
    out_wide = grad_out.astype(jnp.float32)
    query = qkv_saved[:, 0, :].astype(jnp.float32)
    key_part = qkv_saved[:, 1, :].astype(jnp.float32)
    value_part = qkv_saved[:, 2, :].astype(jnp.float32)
    grad_query = out_wide * conv_saved.astype(jnp.float32)
    grad_mixed = lax.optimization_barrier((out_wide * query).astype(jnp.bfloat16)).astype(jnp.float32)
    filters = jnp.repeat(long_taps.astype(jnp.float32), GROUP, axis=1)
    blocks = 8
    piece = D // blocks
    grads_split = grad_mixed.reshape(TOKENS, blocks, piece).transpose(1, 0, 2)
    filters_split = filters.reshape(TOKENS, blocks, piece).transpose(1, 0, 2)
    grad_z = lax.map(correlate_block, (grads_split, filters_split))
    grad_z = grad_z.transpose(1, 0, 2).reshape(TOKENS, D)
    grad_key = grad_z * value_part
    grad_value = grad_z * key_part
    stacked = jnp.stack([grad_query, grad_key, grad_value], 1)
    extended = jnp.concatenate([stacked, jnp.zeros((SHORT - 1, 3, D), stacked.dtype)], 0)
    result = jnp.zeros_like(stacked)
    for lag_index in range(SHORT):
        result = result + short_taps[:, lag_index, :][None] * extended[lag_index:lag_index + TOKENS]
    return result.astype(jnp.bfloat16)
```

```python
import functools

import jax
import jax.numpy as jnp
from jax import lax
from jax.experimental import pallas as pl
from jax.experimental.pallas import tpu as pltpu
from jax.sharding import PartitionSpec as P

MESH = pl.DeviceIdType.MESH
f32 = jnp.float32
bf16 = jnp.bfloat16

LANES = 128
TILE = 256
PER = 16
SEG = 8


def kernel(
    S, C,
    go_ref, qkv_ref, cv_ref, tp_ref, st_ref, out_ref,
    tap_send, tap_recv, rev_ref, strip, x_send, x_recv, acc, y_send, y_recv,
    eq, ez, wq, wz,
    tap_sem, x_ssem, x_rsem, y_ssem, y_rsem, h_ssem, h_rsem, o_ssem, o_rsem,
):
    rows, channels = go_ref.shape
    half = channels // 2
    tiles = S * rows // TILE
    own = rows // TILE
    part = rows // C
    me_s = lax.axis_index("seq")
    me_c = lax.axis_index("chan")

    def local(src, dst, sem):
        pltpu.make_async_copy(src, dst, sem).start()

    def landed(ref, sem):
        pltpu.make_async_copy(ref, ref, sem).wait()

    def seq_copy(src, dst, ssem, rsem, j):
        return pltpu.make_async_remote_copy(
            src_ref=src, dst_ref=dst, send_sem=ssem, recv_sem=rsem,
            device_id=(j, me_c), device_id_type=MESH,
        )

    def chan_copy(src, dst, ssem, rsem, j):
        return pltpu.make_async_remote_copy(
            src_ref=src, dst_ref=dst, send_sem=ssem, recv_sem=rsem,
            device_id=(me_s, j), device_id_type=MESH,
        )

    barrier = pltpu.get_barrier_semaphore()

    def greet_seq(k, carry):
        pl.semaphore_signal(barrier, inc=1, device_id=(lax.rem(me_s + k, S), me_c), device_id_type=MESH)
        return carry

    def greet_chan(k, carry):
        pl.semaphore_signal(barrier, inc=1, device_id=(me_s, lax.rem(me_c + k, C)), device_id_type=MESH)
        return carry

    lax.fori_loop(1, S, greet_seq, 0)
    lax.fori_loop(1, C, greet_chan, 0)

    quarters = rows // LANES
    for g in range(2):
        for q in range(quarters):
            tap_send[:, g * quarters + q, :] = tp_ref[g * S:(g + 1) * S, q * LANES:(q + 1) * LANES].astype(f32)

    def mix(g):
        cols = slice(g * half, (g + 1) * half)
        gm = (go_ref[:, cols].astype(f32) * qkv_ref[0, :, cols].astype(f32)).astype(bf16)
        turned = gm.T
        for h in range(own):
            x_send[g, :, h] = turned[:, h * TILE:(h + 1) * TILE].reshape(S, PER, TILE)

    mix(0)
    pl.semaphore_wait(barrier, S + C - 2)

    local(tap_send.at[me_s], tap_recv.at[me_s], tap_sem.at[1])

    def push_taps(k, carry):
        j = lax.rem(me_s + k, S)
        seq_copy(tap_send.at[j], tap_recv.at[me_s], tap_sem.at[0], tap_sem.at[1], j).start()
        return carry

    lax.fori_loop(1, S, push_taps, 0)

    def push_x(g):
        mine = pl.ds(me_s * own, own)
        local(x_send.at[g, me_s], x_recv.at[g, mine], x_rsem.at[g])

        def push(k, carry):
            j = lax.rem(me_s + k, S)
            seq_copy(x_send.at[g, j], x_recv.at[g, mine], x_ssem.at[g], x_rsem.at[g], j).start()
            return carry

        lax.fori_loop(1, S, push, 0)

    push_x(0)
    mix(1)
    push_x(1)

    def halo(src, dst, n):
        return seq_copy(src, dst, h_ssem.at[n], h_rsem.at[n], lax.rem(me_s + S - 1, S))

    def push_halo(src, dst, n):
        @pl.when(me_s > 0)
        def _():
            halo(src, dst, n).start()

        @pl.when(me_s == S - 1)
        def _():
            dst[...] = jnp.zeros(dst.shape, dst.dtype)

    def wait_halo(src, dst, n):
        @pl.when(me_s < S - 1)
        def _():
            halo(src, dst, n).wait_recv()

    def wait_halo_sent(src, dst, n):
        @pl.when(me_s > 0)
        def _():
            halo(src, dst, n).wait_send()

    def taps3(e, first, taps):
        block = e[pl.ds(first, part + 8), :]
        return taps[0:1] * block[0:part] + taps[1:2] * block[1:part + 1] + taps[2:3] * block[2:part + 2]

    def chan_chunks(body):
        def step(k, carry):
            body(lax.rem(me_c + k, C - 1))
            return carry

        lax.fori_loop(0, C - 1, step, 0)

    eq[0:rows, :] = go_ref[...].astype(f32) * cv_ref[...].astype(f32)
    q_src, q_dst = eq.at[0:8, :], eq.at[rows:rows + 8, :]
    push_halo(q_src, q_dst, 0)

    def query_chunk(c):
        first = pl.multiple_of(c * part, part)
        at = pl.ds(first, part)
        wq[at, :] = taps3(eq, first, st_ref[0]).astype(bf16)
        dst = out_ref.at[0, :, pl.ds(pl.multiple_of(me_c * channels, channels), channels)]

        @pl.when(c == me_c)
        def _():
            local(wq.at[at, :], dst, o_rsem.at[2])

        @pl.when(c != me_c)
        def _():
            chan_copy(wq.at[at, :], dst, o_ssem.at[2], o_rsem.at[2], c).start()

    chan_chunks(query_chunk)
    wait_halo(q_src, q_dst, 0)
    query_chunk(C - 1)

    landed(tap_recv, tap_sem.at[1])
    down = lax.broadcasted_iota(jnp.int32, (LANES, LANES), 0)
    over = lax.broadcasted_iota(jnp.int32, (LANES, LANES), 1)
    mirror = (lax.rem(down + over, LANES) == 0).astype(f32).astype(bf16)
    rev = jnp.dot(
        tap_recv[...].reshape(S * 2 * quarters, LANES).astype(bf16), mirror, preferred_element_type=f32
    )
    rev_ref[...] = rev.reshape(S, 2, quarters, LANES)
    newer = (over == 0) | (over >= LANES - down)

    def grow(s, before):
        after = []
        for g in range(2):
            last = before[g]
            for q in range(quarters):
                row = rev_ref[s, g, q:q + 1, :]
                mixed = jnp.where(newer, jnp.broadcast_to(row, (LANES, LANES)), jnp.broadcast_to(last, (LANES, LANES)))
                rolled = pltpu.roll(mixed, 0, 1, stride=1, stride_axis=0)
                at = pl.multiple_of((s * quarters + q + 1) * LANES, LANES)
                strip[g, pl.ds(at, LANES), :] = rolled.astype(bf16)
                last = row
            after.append(last)
        return tuple(after)

    strip[:, 0:LANES, :] = jnp.zeros((2, LANES, LANES), bf16)
    nothing = jnp.zeros((1, LANES), f32)
    lax.fori_loop(0, S, grow, (nothing, nothing))

    for g in range(2):
        x_recv[g, tiles:tiles + SEG - 1] = jnp.zeros((SEG - 1, PER, TILE), bf16)

    def correlate(g):
        landed(x_recv.at[g, 0:tiles], x_rsem.at[g])
        for seg in range(tiles // SEG):
            n = tiles - seg * SEG
            deep = SEG * TILE
            left = jnp.concatenate(
                [x_recv[g, seg * SEG + d:seg * SEG + d + n].reshape(n * PER, TILE) for d in range(SEG)], 1
            )
            right = jnp.concatenate(
                [
                    strip[g, LANES + seg * deep:LANES + (seg + 1) * deep, :],
                    strip[g, seg * deep:(seg + 1) * deep, :],
                ],
                1,
            )
            product = jnp.dot(left, right, preferred_element_type=f32)
            if seg == 0:
                acc[...] = product
            else:
                acc[0:n * PER, :] += product
        y_send[g] = acc[...].astype(bf16).reshape(tiles, PER, TILE)
        local(y_send.at[g, pl.ds(me_s * own, own)], y_recv.at[g, me_s], y_rsem.at[g])

        def push(k, carry):
            j = lax.rem(me_s + k, S)
            seq_copy(
                y_send.at[g, pl.ds(j * own, own)], y_recv.at[g, me_s], y_ssem.at[g], y_rsem.at[g], j
            ).start()
            return carry

        lax.fori_loop(1, S, push, 0)

    correlate(0)
    correlate(1)

    def finish(g):
        cols = slice(g * half, (g + 1) * half)
        landed(y_recv.at[g], y_rsem.at[g])
        for h in range(own):
            at = slice(h * TILE, (h + 1) * TILE)
            gz = y_recv[g, :, h].reshape(half, TILE).T.astype(f32)
            ez[g, 0, at, :] = gz * qkv_ref[2, at, cols].astype(f32)
            ez[g, 1, at, :] = gz * qkv_ref[1, at, cols].astype(f32)
        src, dst = ez.at[g, :, 0:8, :], ez.at[g, :, rows:rows + 8, :]
        push_halo(src, dst, 1 + g)

        def chunk(c):
            first = pl.multiple_of(c * part, part)
            at = pl.ds(first, part)
            for p in range(2):
                wz[g, p, at, :] = taps3(ez.at[g, p], first, st_ref[1 + p, :, cols]).astype(bf16)
            block = wz.at[g, :, at, :]
            to = out_ref.at[1:3, :, pl.ds(pl.multiple_of(me_c * channels + g * half, half), half)]

            @pl.when(c == me_c)
            def _():
                local(block, to, o_rsem.at[g])

            @pl.when(c != me_c)
            def _():
                chan_copy(block, to, o_ssem.at[g], o_rsem.at[g], c).start()

        chan_chunks(chunk)
        wait_halo(src, dst, 1 + g)
        chunk(C - 1)

    finish(0)
    finish(1)

    landed(out_ref.at[0], o_rsem.at[2])
    for g in range(2):
        landed(out_ref.at[1:3, :, 0:C * half], o_rsem.at[g])

    landed(tap_send.at[0:S - 1], tap_sem.at[0])
    landed(wq.at[0:rows - part, :], o_ssem.at[2])
    wait_halo_sent(q_src, q_dst, 0)
    for g in range(2):
        landed(x_send.at[g, 0:S - 1], x_ssem.at[g])
        landed(y_send.at[g, 0:tiles - own], y_ssem.at[g])
        landed(wz.at[g, :, 0:rows - part, :], o_ssem.at[g])
        wait_halo_sent(ez.at[g, :, 0:8, :], ez.at[g, :, rows:rows + 8, :], 1 + g)


def on_device(S, C, grad_out, qkv_saved, conv_saved, long_taps, short_taps):
    rows, channels = grad_out.shape
    half = channels // 2
    tiles = S * rows // TILE
    own = rows // TILE
    quarters = rows // LANES
    vmem = pl.BlockSpec(memory_space=pltpu.VMEM)
    out = pl.pallas_call(
        functools.partial(kernel, S, C),
        out_shape=jax.ShapeDtypeStruct((3, rows // C, C * channels), bf16),
        in_specs=[vmem] * 5,
        out_specs=pl.BlockSpec(memory_space=pl.ANY),
        scratch_shapes=[
            pltpu.VMEM((S, 2 * quarters, LANES), f32),
            pltpu.VMEM((S, 2 * quarters, LANES), f32),
            pltpu.VMEM((S, 2, quarters, LANES), f32),
            pltpu.VMEM((2, LANES + tiles * TILE, LANES), bf16),
            pltpu.VMEM((2, S, own, PER, TILE), bf16),
            pltpu.VMEM((2, tiles + SEG, PER, TILE), bf16),
            pltpu.VMEM((tiles * PER, TILE), f32),
            pltpu.VMEM((2, tiles, PER, TILE), bf16),
            pltpu.VMEM((2, S, own, PER, TILE), bf16),
            pltpu.VMEM((rows + 8, channels), f32),
            pltpu.VMEM((2, 2, rows + 8, half), f32),
            pltpu.VMEM((rows, channels), bf16),
            pltpu.VMEM((2, 2, rows, half), bf16),
            pltpu.SemaphoreType.DMA((2,)),
            pltpu.SemaphoreType.DMA((2,)),
            pltpu.SemaphoreType.DMA((2,)),
            pltpu.SemaphoreType.DMA((2,)),
            pltpu.SemaphoreType.DMA((2,)),
            pltpu.SemaphoreType.DMA((3,)),
            pltpu.SemaphoreType.DMA((3,)),
            pltpu.SemaphoreType.DMA((3,)),
            pltpu.SemaphoreType.DMA((3,)),
        ],
        compiler_params=pltpu.CompilerParams(
            collective_id=0, has_side_effects=True, vmem_limit_bytes=48 * 1024 * 1024
        ),
    )(grad_out, qkv_saved.transpose(1, 0, 2), conv_saved, long_taps.T, short_taps)
    return out.transpose(1, 0, 2)


def solution(mesh):
    in_specs = (
        P("seq", "chan"),
        P("seq", None, "chan"),
        P("seq", "chan"),
        P("seq", "chan"),
        P(None, None, "chan"),
    )
    out_specs = P(("seq", "chan"), None, None)
    return jax.shard_map(
        functools.partial(on_device, mesh.shape["seq"], mesh.shape["chan"]),
        mesh=mesh, in_specs=in_specs, out_specs=out_specs, check_vma=False,
    )
```

```python
import functools
import math

import jax
import jax.numpy as jnp
from jax import lax
from jax.experimental import pallas as pl
from jax.experimental.pallas import tpu as pltpu
from jax.sharding import PartitionSpec as P

MESH = pl.DeviceIdType.MESH
f32 = jnp.float32
bf16 = jnp.bfloat16

LANES = 128
TILE = 256
PER = 16
SEG = 8


def kernel(
    S, C,
    go_hbm, qkv_hbm, cv_hbm, tp_hbm, st_hbm, out_ref,
    go_ref, qkv_ref, cv_ref, tp_ref, st_ref, in_sem,
    tap_send, tap_recv, rev_ref, strip, x_send, x_recv, acc, y_send, y_recv,
    eq, ez, wq, wz,
    tap_sem, x_ssem, x_rsem, y_ssem, y_rsem, h_ssem, h_rsem, o_ssem, o_rsem,
):
    rows, channels = go_ref.shape
    half = channels // 2
    tiles = S * rows // TILE
    own = rows // TILE
    part = rows // C
    me_s = lax.axis_index("seq")
    me_c = lax.axis_index("chan")

    def local(src, dst, sem):
        pltpu.make_async_copy(src, dst, sem).start()

    def landed(ref, sem):
        pltpu.make_async_copy(ref, ref, sem).wait()

    def seq_copy(src, dst, ssem, rsem, j):
        return pltpu.make_async_remote_copy(
            src_ref=src, dst_ref=dst, send_sem=ssem, recv_sem=rsem,
            device_id=(j, me_c), device_id_type=MESH,
        )

    def chan_copy(src, dst, ssem, rsem, j):
        return pltpu.make_async_remote_copy(
            src_ref=src, dst_ref=dst, send_sem=ssem, recv_sem=rsem,
            device_id=(me_s, j), device_id_type=MESH,
        )

    turn = 1 - 2 * lax.rem(me_s, 2)
    if S % 2 == 0:
        chips = S // 2
        steps = sorted(range(1, chips), key=lambda z: -min(z, chips - z))
        seq_order = [
            lax.rem(me_s // 2 + turn * z + chips, chips) * 2 + lax.rem(me_s + core, 2) for z in steps for core in range(2)
        ] + [me_s + turn]
    else:
        seq_order = [lax.rem(me_s + k, S) for k in range(1, S)]
    side = math.isqrt(C)
    if side * side == C:
        moves = sorted(
            [(x, y) for x in range(side) for y in range(side) if x + y > 0],
            key=lambda m: -(min(m[0], side - m[0]) + min(m[1], side - m[1])),
        )
        chan_order = [
            lax.rem(me_c // side + turn * x + side, side) * side + lax.rem(lax.rem(me_c, side) + turn * y + side, side)
            for x, y in moves
        ]
    else:
        chan_order = [lax.rem(me_c + k, C) for k in range(1, C)]

    loads = {}

    def load(name, src, dst):
        loads[name] = pltpu.make_async_copy(src, dst, in_sem.at[len(loads)])
        loads[name].start()

    for g in range(2):
        cols = slice(g * half, (g + 1) * half)
        load(f"go{g}", go_hbm.at[:, cols], go_ref.at[:, cols])
        load(f"q{g}", qkv_hbm.at[0, :, cols], qkv_ref.at[0, :, cols])
        if g == 0:
            load("tp", tp_hbm, tp_ref)
    load("cv", cv_hbm, cv_ref)
    load("st", st_hbm, st_ref)
    load("kv", qkv_hbm.at[1:3], qkv_ref.at[1:3])

    barrier = pltpu.get_barrier_semaphore()

    def greet_seq(k, carry):
        pl.semaphore_signal(barrier, inc=1, device_id=(lax.rem(me_s + k, S), me_c), device_id_type=MESH)
        return carry

    def greet_chan(k, carry):
        pl.semaphore_signal(barrier, inc=1, device_id=(me_s, lax.rem(me_c + k, C)), device_id_type=MESH)
        return carry

    lax.fori_loop(1, S, greet_seq, 0)
    lax.fori_loop(1, C, greet_chan, 0)

    quarters = rows // LANES
    loads["tp"].wait()
    for g in range(2):
        for q in range(quarters):
            tap_send[:, g * quarters + q, :] = tp_ref[g * S:(g + 1) * S, q * LANES:(q + 1) * LANES].astype(f32)

    def mix(g):
        cols = slice(g * half, (g + 1) * half)
        loads[f"go{g}"].wait()
        loads[f"q{g}"].wait()
        gm = (go_ref[:, cols].astype(f32) * qkv_ref[0, :, cols].astype(f32)).astype(bf16)
        turned = gm.T
        for h in range(own):
            x_send[g, :, h] = turned[:, h * TILE:(h + 1) * TILE].reshape(S, PER, TILE)

    mix(0)
    pl.semaphore_wait(barrier, S + C - 2)

    local(tap_send.at[me_s], tap_recv.at[me_s], tap_sem.at[1])

    for j in seq_order:
        seq_copy(tap_send.at[j], tap_recv.at[me_s], tap_sem.at[0], tap_sem.at[1], j).start()

    def push_x(g):
        mine = pl.ds(me_s * own, own)
        local(x_send.at[g, me_s], x_recv.at[g, mine], x_rsem.at[g])

        for j in seq_order:
            seq_copy(x_send.at[g, j], x_recv.at[g, mine], x_ssem.at[g], x_rsem.at[g], j).start()

    push_x(0)
    mix(1)
    push_x(1)

    def halo(src, dst, n):
        return seq_copy(src, dst, h_ssem.at[n], h_rsem.at[n], lax.rem(me_s + S - 1, S))

    def push_halo(src, dst, n):
        @pl.when(me_s > 0)
        def _():
            halo(src, dst, n).start()

        @pl.when(me_s == S - 1)
        def _():
            dst[...] = jnp.zeros(dst.shape, dst.dtype)

    def wait_halo(src, dst, n):
        @pl.when(me_s < S - 1)
        def _():
            halo(src, dst, n).wait_recv()

    def wait_halo_sent(src, dst, n):
        @pl.when(me_s > 0)
        def _():
            halo(src, dst, n).wait_send()

    def taps3(e, first, taps):
        return sum(taps[j:j + 1] * e[first + j:first + j + part, :] for j in range(3))

    def spread(source, dst, ssem, rsem, blocks):
        def send(c):
            block = source(pl.ds(pl.multiple_of(c * part, part), part))

            @pl.when(c == me_c)
            def _():
                local(block, dst, rsem)

            @pl.when(c != me_c)
            def _():
                chan_copy(block, dst, ssem, rsem, c).start()

        if blocks == "last":
            send(C - 1)
            return
        for c in chan_order:

            @pl.when(c < C - 1)
            def _(c=c):
                chan_copy(source(pl.ds(pl.multiple_of(c * part, part), part)), dst, ssem, rsem, c).start()

        @pl.when(me_c < C - 1)
        def _():
            local(source(pl.ds(pl.multiple_of(me_c * part, part), part)), dst, rsem)

    loads["cv"].wait()
    loads["st"].wait()
    eq[0:rows, :] = go_ref[...].astype(f32) * cv_ref[...].astype(f32)
    q_src, q_dst = eq.at[0:8, :], eq.at[rows:rows + 8, :]
    push_halo(q_src, q_dst, 0)

    def query(blocks):
        for c in range(C - 1) if blocks == "first" else [C - 1]:
            wq[c * part:(c + 1) * part, :] = taps3(eq, c * part, st_ref[0]).astype(bf16)
        dst = out_ref.at[0, :, pl.ds(pl.multiple_of(me_c * channels, channels), channels)]
        spread(lambda at: wq.at[at, :], dst, o_ssem.at[2], o_rsem.at[2], blocks)

    query("first")

    landed(tap_recv, tap_sem.at[1])
    down = lax.broadcasted_iota(jnp.int32, (LANES, LANES), 0)
    over = lax.broadcasted_iota(jnp.int32, (LANES, LANES), 1)
    mirror = (lax.rem(down + over, LANES) == 0).astype(f32).astype(bf16)
    rev = jnp.dot(
        tap_recv[...].reshape(S * 2 * quarters, LANES).astype(bf16), mirror, preferred_element_type=f32
    )
    rev_ref[...] = rev.reshape(S, 2, quarters, LANES)
    newer = (over == 0) | (over >= LANES - down)

    def grow(s, before):
        after = []
        for g in range(2):
            last = before[g]
            for q in range(quarters):
                row = rev_ref[s, g, q:q + 1, :]
                mixed = jnp.where(newer, jnp.broadcast_to(row, (LANES, LANES)), jnp.broadcast_to(last, (LANES, LANES)))
                rolled = pltpu.roll(mixed, 0, 1, stride=1, stride_axis=0)
                at = pl.multiple_of((s * quarters + q + 1) * LANES, LANES)
                strip[g, pl.ds(at, LANES), :] = rolled.astype(bf16)
                last = row
            after.append(last)
        return tuple(after)

    strip[:, 0:LANES, :] = jnp.zeros((2, LANES, LANES), bf16)
    nothing = jnp.zeros((1, LANES), f32)
    lax.fori_loop(0, S, grow, (nothing, nothing))

    for g in range(2):
        x_recv[g, tiles:tiles + SEG - 1] = jnp.zeros((SEG - 1, PER, TILE), bf16)

    def correlate(g):
        landed(x_recv.at[g, 0:tiles], x_rsem.at[g])
        for seg in range(tiles // SEG):
            n = tiles - seg * SEG
            deep = SEG * TILE
            left = jnp.concatenate(
                [x_recv[g, seg * SEG + d:seg * SEG + d + n].reshape(n * PER, TILE) for d in range(SEG)], 1
            )
            right = jnp.concatenate(
                [
                    strip[g, LANES + seg * deep:LANES + (seg + 1) * deep, :],
                    strip[g, seg * deep:(seg + 1) * deep, :],
                ],
                1,
            )
            product = jnp.dot(left, right, preferred_element_type=f32)
            if seg == 0:
                acc[...] = product
            else:
                acc[0:n * PER, :] += product
        y_send[g] = acc[...].astype(bf16).reshape(tiles, PER, TILE)
        local(y_send.at[g, pl.ds(me_s * own, own)], y_recv.at[g, me_s], y_rsem.at[g])

        for j in seq_order:
            seq_copy(
                y_send.at[g, pl.ds(j * own, own)], y_recv.at[g, me_s], y_ssem.at[g], y_rsem.at[g], j
            ).start()

    correlate(0)
    wait_halo(q_src, q_dst, 0)
    query("last")
    correlate(1)

    def weigh(g, blocks):
        cols = slice(g * half, (g + 1) * half)
        for c in range(C - 1) if blocks == "first" else [C - 1]:
            for p in range(2):
                wz[g, p, c * part:(c + 1) * part, :] = taps3(
                    ez.at[g, p], c * part, st_ref[1 + p, :, cols]
                ).astype(bf16)
        dst = out_ref.at[1:3, :, pl.ds(pl.multiple_of(me_c * channels + g * half, half), half)]
        spread(lambda at: wz.at[g, :, at, :], dst, o_ssem.at[g], o_rsem.at[g], blocks)

    def halo_ends(g):
        return ez.at[g, :, 0:8, :], ez.at[g, :, rows:rows + 8, :]

    def finish(g):
        cols = slice(g * half, (g + 1) * half)
        landed(y_recv.at[g], y_rsem.at[g])
        for h in range(own):
            at = slice(h * TILE, (h + 1) * TILE)
            gz = y_recv[g, :, h].reshape(half, TILE).T.astype(f32)
            ez[g, 0, at, :] = gz * qkv_ref[2, at, cols].astype(f32)
            ez[g, 1, at, :] = gz * qkv_ref[1, at, cols].astype(f32)
            if h == 0:
                push_halo(*halo_ends(g), 1 + g)
        weigh(g, "first")

    loads["kv"].wait()
    finish(0)
    finish(1)
    for g in range(2):
        wait_halo(*halo_ends(g), 1 + g)
        weigh(g, "last")

    landed(out_ref.at[0], o_rsem.at[2])
    for g in range(2):
        landed(out_ref.at[1:3, :, 0:C * half], o_rsem.at[g])

    landed(tap_send.at[0:S - 1], tap_sem.at[0])
    landed(wq.at[0:rows - part, :], o_ssem.at[2])
    wait_halo_sent(q_src, q_dst, 0)
    for g in range(2):
        landed(x_send.at[g, 0:S - 1], x_ssem.at[g])
        landed(y_send.at[g, 0:tiles - own], y_ssem.at[g])
        landed(wz.at[g, :, 0:rows - part, :], o_ssem.at[g])
        wait_halo_sent(*halo_ends(g), 1 + g)


def on_device(S, C, grad_out, qkv_saved, conv_saved, long_taps, short_taps):
    rows, channels = grad_out.shape
    half = channels // 2
    tiles = S * rows // TILE
    own = rows // TILE
    quarters = rows // LANES
    out = pl.pallas_call(
        functools.partial(kernel, S, C),
        out_shape=jax.ShapeDtypeStruct((3, rows // C, C * channels), bf16),
        in_specs=[pl.BlockSpec(memory_space=pltpu.HBM)] * 5,
        out_specs=pl.BlockSpec(memory_space=pl.ANY),
        scratch_shapes=[
            pltpu.VMEM((rows, channels), bf16),
            pltpu.VMEM((3, rows, channels), bf16),
            pltpu.VMEM((rows, channels), bf16),
            pltpu.VMEM((2 * S, rows), bf16),
            pltpu.VMEM((3, 3, channels), f32),
            pltpu.SemaphoreType.DMA((8,)),
            pltpu.VMEM((S, 2 * quarters, LANES), f32),
            pltpu.VMEM((S, 2 * quarters, LANES), f32),
            pltpu.VMEM((S, 2, quarters, LANES), f32),
            pltpu.VMEM((2, LANES + tiles * TILE, LANES), bf16),
            pltpu.VMEM((2, S, own, PER, TILE), bf16),
            pltpu.VMEM((2, tiles + SEG, PER, TILE), bf16),
            pltpu.VMEM((tiles * PER, TILE), f32),
            pltpu.VMEM((2, tiles, PER, TILE), bf16),
            pltpu.VMEM((2, S, own, PER, TILE), bf16),
            pltpu.VMEM((rows + 8, channels), f32),
            pltpu.VMEM((2, 2, rows + 8, half), f32),
            pltpu.VMEM((rows, channels), bf16),
            pltpu.VMEM((2, 2, rows, half), bf16),
            pltpu.SemaphoreType.DMA((2,)),
            pltpu.SemaphoreType.DMA((2,)),
            pltpu.SemaphoreType.DMA((2,)),
            pltpu.SemaphoreType.DMA((2,)),
            pltpu.SemaphoreType.DMA((2,)),
            pltpu.SemaphoreType.DMA((3,)),
            pltpu.SemaphoreType.DMA((3,)),
            pltpu.SemaphoreType.DMA((3,)),
            pltpu.SemaphoreType.DMA((3,)),
        ],
        compiler_params=pltpu.CompilerParams(
            collective_id=0, has_side_effects=True, vmem_limit_bytes=48 * 1024 * 1024
        ),
    )(*[
        pltpu.with_memory_space_constraint(value, pltpu.HBM)
        for value in (grad_out, qkv_saved.transpose(1, 0, 2), conv_saved, long_taps.T, short_taps)
    ])
    return out.transpose(1, 0, 2)


def solution(mesh):
    in_specs = (
        P("seq", "chan"),
        P("seq", None, "chan"),
        P("seq", "chan"),
        P("seq", "chan"),
        P(None, None, "chan"),
    )
    out_specs = P(("seq", "chan"), None, None)
    return jax.shard_map(
        functools.partial(on_device, mesh.shape["seq"], mesh.shape["chan"]),
        mesh=mesh, in_specs=in_specs, out_specs=out_specs, check_vma=False,
    )
```

```python
import functools
import math

import jax
import jax.numpy as jnp
from jax import lax
from jax.experimental import pallas as pl
from jax.experimental.pallas import tpu as pltpu
from jax.sharding import PartitionSpec as P

MESH = pl.DeviceIdType.MESH
f32 = jnp.float32
bf16 = jnp.bfloat16

LANES = 128
TILE = 256
PER = 16
SEG = 8


def kernel(
    S, C,
    go_hbm, qkv_hbm, cv_hbm, tp_hbm, st_hbm, out_ref,
    go_ref, qkv_ref, cv_ref, tp_ref, st_ref, in_sem,
    tap_send, tap_recv, rev_ref, strip, x_send, x_recv, acc, y_send, y_recv,
    edge_send, edge_recv, kv_edge, eq, ez, wq, wz,
    tap_sem, x_ssem, x_rsem, y_ssem, y_rsem, e_ssem, e_rsem, h_ssem, h_rsem, o_ssem, o_rsem,
):
    rows, channels = go_ref.shape
    half = channels // 2
    tiles = S * rows // TILE
    own = rows // TILE
    part = rows // C
    me_s = lax.axis_index("seq")
    me_c = lax.axis_index("chan")

    def local(src, dst, sem):
        pltpu.make_async_copy(src, dst, sem).start()

    def landed(ref, sem):
        pltpu.make_async_copy(ref, ref, sem).wait()

    def seq_copy(src, dst, ssem, rsem, j):
        return pltpu.make_async_remote_copy(
            src_ref=src, dst_ref=dst, send_sem=ssem, recv_sem=rsem,
            device_id=(j, me_c), device_id_type=MESH,
        )

    def chan_copy(src, dst, ssem, rsem, j):
        return pltpu.make_async_remote_copy(
            src_ref=src, dst_ref=dst, send_sem=ssem, recv_sem=rsem,
            device_id=(me_s, j), device_id_type=MESH,
        )

    turn = 1 - 2 * lax.rem(me_s, 2)
    if S % 2 == 0:
        chips = S // 2
        steps = sorted(range(1, chips), key=lambda z: -min(z, chips - z))
        seq_order = [
            lax.rem(me_s // 2 + turn * z + chips, chips) * 2 + lax.rem(me_s + core, 2) for z in steps for core in range(2)
        ] + [me_s + turn]
    else:
        seq_order = [lax.rem(me_s + k, S) for k in range(1, S)]
    side = math.isqrt(C)
    if side * side == C:
        moves = sorted(
            [(x, y) for x in range(side) for y in range(side) if x + y > 0],
            key=lambda m: -(min(m[0], side - m[0]) + min(m[1], side - m[1])),
        )
        chan_order = [
            lax.rem(me_c // side + turn * x + side, side) * side + lax.rem(lax.rem(me_c, side) + turn * y + side, side)
            for x, y in moves
        ]
    else:
        chan_order = [lax.rem(me_c + k, C) for k in range(1, C)]

    loads = {}

    def load(name, src, dst):
        loads[name] = pltpu.make_async_copy(src, dst, in_sem.at[len(loads)])
        loads[name].start()

    for g in range(2):
        cols = slice(g * half, (g + 1) * half)
        load(f"go{g}", go_hbm.at[:, cols], go_ref.at[:, cols])
        load(f"q{g}", qkv_hbm.at[0, :, cols], qkv_ref.at[0, :, cols])
        if g == 0:
            load("tp", tp_hbm, tp_ref)
    load("cv", cv_hbm, cv_ref)
    load("st", st_hbm, st_ref)
    load("kv", qkv_hbm.at[1:3], qkv_ref.at[1:3])

    barrier = pltpu.get_barrier_semaphore()

    def greet_seq(k, carry):
        pl.semaphore_signal(barrier, inc=1, device_id=(lax.rem(me_s + k, S), me_c), device_id_type=MESH)
        return carry

    def greet_chan(k, carry):
        pl.semaphore_signal(barrier, inc=1, device_id=(me_s, lax.rem(me_c + k, C)), device_id_type=MESH)
        return carry

    lax.fori_loop(1, S, greet_seq, 0)
    lax.fori_loop(1, C, greet_chan, 0)

    quarters = rows // LANES
    loads["tp"].wait()
    for g in range(2):
        for q in range(quarters):
            tap_send[:, g * quarters + q, :] = tp_ref[g * S:(g + 1) * S, q * LANES:(q + 1) * LANES].astype(f32)

    def mix(g):
        cols = slice(g * half, (g + 1) * half)
        loads[f"go{g}"].wait()
        loads[f"q{g}"].wait()
        gm = (go_ref[:, cols].astype(f32) * qkv_ref[0, :, cols].astype(f32)).astype(bf16)
        turned = gm.T
        for h in range(own):
            x_send[g, :, h] = turned[:, h * TILE:(h + 1) * TILE].reshape(S, PER, TILE)

    mix(0)
    pl.semaphore_wait(barrier, S + C - 2)

    local(tap_send.at[me_s], tap_recv.at[me_s], tap_sem.at[1])

    for j in seq_order:
        seq_copy(tap_send.at[j], tap_recv.at[me_s], tap_sem.at[0], tap_sem.at[1], j).start()

    def push_x(g):
        mine = pl.ds(me_s * own, own)
        local(x_send.at[g, me_s], x_recv.at[g, mine], x_rsem.at[g])

        for j in seq_order:
            seq_copy(x_send.at[g, j], x_recv.at[g, mine], x_ssem.at[g], x_rsem.at[g], j).start()

    push_x(0)
    mix(1)
    push_x(1)

    loads["kv"].wait()
    kv_copy = seq_copy(
        qkv_ref.at[1:3, 0:PER, :], kv_edge, h_ssem.at[1], h_rsem.at[1], lax.rem(me_s + S - 1, S)
    )
    kv_copy.start()

    def halo(src, dst, n):
        return seq_copy(src, dst, h_ssem.at[n], h_rsem.at[n], lax.rem(me_s + S - 1, S))

    def push_halo(src, dst, n):
        @pl.when(me_s > 0)
        def _():
            halo(src, dst, n).start()

        @pl.when(me_s == S - 1)
        def _():
            dst[...] = jnp.zeros(dst.shape, dst.dtype)

    def wait_halo(src, dst, n):
        @pl.when(me_s < S - 1)
        def _():
            halo(src, dst, n).wait_recv()

    def wait_halo_sent(src, dst, n):
        @pl.when(me_s > 0)
        def _():
            halo(src, dst, n).wait_send()

    def taps3(e, first, taps):
        return sum(taps[j:j + 1] * e[first + j:first + j + part, :] for j in range(3))

    def spread(source, dst, ssem, rsem, late):
        def block(c):
            return source(pl.ds(pl.multiple_of(c * part, part), part))

        def fits(c):
            return c >= 0 if late is None else (c == C - 1 if late else c < C - 1)

        for c in chan_order:

            @pl.when(fits(c))
            def _(c=c):
                chan_copy(block(c), dst, ssem, rsem, c).start()

        @pl.when(fits(me_c))
        def _():
            local(block(me_c), dst, rsem)

    loads["cv"].wait()
    loads["st"].wait()
    eq[0:rows, :] = go_ref[...].astype(f32) * cv_ref[...].astype(f32)
    q_src, q_dst = eq.at[0:8, :], eq.at[rows:rows + 8, :]
    push_halo(q_src, q_dst, 0)

    def query(blocks):
        for c in range(C - 1) if blocks == "first" else [C - 1]:
            wq[c * part:(c + 1) * part, :] = taps3(eq, c * part, st_ref[0]).astype(bf16)
        dst = out_ref.at[0, :, pl.ds(pl.multiple_of(me_c * channels, channels), channels)]
        spread(lambda at: wq.at[at, :], dst, o_ssem.at[2], o_rsem.at[2], blocks == "last")

    query("first")

    landed(tap_recv, tap_sem.at[1])
    down = lax.broadcasted_iota(jnp.int32, (LANES, LANES), 0)
    over = lax.broadcasted_iota(jnp.int32, (LANES, LANES), 1)
    mirror = (lax.rem(down + over, LANES) == 0).astype(f32).astype(bf16)
    rev = jnp.dot(
        tap_recv[...].reshape(S * 2 * quarters, LANES).astype(bf16), mirror, preferred_element_type=f32
    )
    rev_ref[...] = rev.reshape(S, 2, quarters, LANES)
    newer = (over == 0) | (over >= LANES - down)

    def grow(s, before):
        after = []
        for g in range(2):
            last = before[g]
            for q in range(quarters):
                row = rev_ref[s, g, q:q + 1, :]
                mixed = jnp.where(newer, jnp.broadcast_to(row, (LANES, LANES)), jnp.broadcast_to(last, (LANES, LANES)))
                rolled = pltpu.roll(mixed, 0, 1, stride=1, stride_axis=0)
                at = pl.multiple_of((s * quarters + q + 1) * LANES, LANES)
                strip[g, pl.ds(at, LANES), :] = rolled.astype(bf16)
                last = row
            after.append(last)
        return tuple(after)

    strip[:, 0:LANES, :] = jnp.zeros((2, LANES, LANES), bf16)
    nothing = jnp.zeros((1, LANES), f32)
    lax.fori_loop(0, S, grow, (nothing, nothing))

    for g in range(2):
        x_recv[g, tiles:tiles + SEG - 1] = jnp.zeros((SEG - 1, PER, TILE), bf16)

    def correlate(g):
        landed(x_recv.at[g, 0:tiles], x_rsem.at[g])
        for seg in range(tiles // SEG):
            n = tiles - seg * SEG
            deep = SEG * TILE
            left = jnp.concatenate(
                [x_recv[g, seg * SEG + d:seg * SEG + d + n].reshape(n * PER, TILE) for d in range(SEG)], 1
            )
            right = jnp.concatenate(
                [
                    strip[g, LANES + seg * deep:LANES + (seg + 1) * deep, :],
                    strip[g, seg * deep:(seg + 1) * deep, :],
                ],
                1,
            )
            product = jnp.dot(left, right, preferred_element_type=f32)
            if seg == 0:
                acc[...] = product
            else:
                acc[0:n * PER, :] += product
        result = acc[...].astype(bf16)
        y_send[g] = result.reshape(tiles, PER, TILE)
        pick = (
            lax.broadcasted_iota(jnp.int32, (8, LANES), 0) == lax.broadcasted_iota(jnp.int32, (8, LANES), 1)
        ).astype(f32).astype(bf16)
        heads = lax.dot_general(
            pick, result[:, 0:LANES], (((1,), (1,)), ((), ())), preferred_element_type=f32
        )
        place = lax.rem(me_s, LANES // PER) * PER
        for j in range(S - 1):
            lane = (j + 1) * own * PER
            base = lane // LANES * LANES
            moved = pltpu.roll(heads[:, base:base + LANES], lax.rem(place + LANES - lane % LANES, LANES), 1)
            edge_send[g, j] = moved[0:2]
        edge_send[g, S - 1] = jnp.zeros((2, LANES), f32)
        local(edge_send.at[g, me_s], edge_recv.at[g, me_s], e_rsem.at[g])
        for j in seq_order:
            seq_copy(edge_send.at[g, j], edge_recv.at[g, me_s], e_ssem.at[g], e_rsem.at[g], j).start()
        local(y_send.at[g, pl.ds(me_s * own, own)], y_recv.at[g, me_s], y_rsem.at[g])

        for j in seq_order:
            seq_copy(
                y_send.at[g, pl.ds(j * own, own)], y_recv.at[g, me_s], y_ssem.at[g], y_rsem.at[g], j
            ).start()

    correlate(0)
    wait_halo(q_src, q_dst, 0)
    query("last")
    correlate(1)

    def finish(g):
        cols = slice(g * half, (g + 1) * half)
        landed(y_recv.at[g], y_rsem.at[g])
        for h in range(own):
            at = slice(h * TILE, (h + 1) * TILE)
            gz = y_recv[g, :, h].reshape(half, TILE).T.astype(f32)
            ez[g, 0, at, :] = gz * qkv_ref[2, at, cols].astype(f32)
            ez[g, 1, at, :] = gz * qkv_ref[1, at, cols].astype(f32)
        landed(edge_recv.at[g], e_rsem.at[g])
        group = lax.broadcasted_iota(jnp.int32, (2, LANES), 1) // PER
        per_tile = LANES // PER
        edges = []
        for tile in range(half // LANES):
            edge = edge_recv[g, tile * per_tile]
            for k in range(1, per_tile):
                edge = jnp.where(group == k, edge_recv[g, tile * per_tile + k], edge)
            edges.append(edge)
        edge = jnp.concatenate(edges, 1)
        ez[g, 0, rows:rows + 2, :] = edge * kv_edge[1, :, cols].astype(f32)[0:2]
        ez[g, 1, rows:rows + 2, :] = edge * kv_edge[0, :, cols].astype(f32)[0:2]
        for c in range(C):
            for p in range(2):
                wz[g, p, c * part:(c + 1) * part, :] = taps3(
                    ez.at[g, p], c * part, st_ref[1 + p, :, cols]
                ).astype(bf16)
        dst = out_ref.at[1:3, :, pl.ds(pl.multiple_of(me_c * channels + g * half, half), half)]
        spread(lambda at: wz.at[g, :, at, :], dst, o_ssem.at[g], o_rsem.at[g], None)

    kv_copy.wait_recv()
    finish(0)
    finish(1)

    landed(out_ref.at[0], o_rsem.at[2])
    for g in range(2):
        landed(out_ref.at[1:3, :, 0:C * half], o_rsem.at[g])

    landed(tap_send.at[0:S - 1], tap_sem.at[0])
    landed(wq.at[0:rows - part, :], o_ssem.at[2])
    wait_halo_sent(q_src, q_dst, 0)
    kv_copy.wait_send()
    for g in range(2):
        landed(x_send.at[g, 0:S - 1], x_ssem.at[g])
        landed(y_send.at[g, 0:tiles - own], y_ssem.at[g])
        landed(wz.at[g, :, 0:rows - part, :], o_ssem.at[g])
        landed(edge_send.at[g, 0:S - 1], e_ssem.at[g])


def on_device(S, C, grad_out, qkv_saved, conv_saved, long_taps, short_taps):
    rows, channels = grad_out.shape
    half = channels // 2
    tiles = S * rows // TILE
    own = rows // TILE
    quarters = rows // LANES
    out = pl.pallas_call(
        functools.partial(kernel, S, C),
        out_shape=jax.ShapeDtypeStruct((3, rows // C, C * channels), bf16),
        in_specs=[pl.BlockSpec(memory_space=pltpu.HBM)] * 5,
        out_specs=pl.BlockSpec(memory_space=pl.ANY),
        scratch_shapes=[
            pltpu.VMEM((rows, channels), bf16),
            pltpu.VMEM((3, rows, channels), bf16),
            pltpu.VMEM((rows, channels), bf16),
            pltpu.VMEM((2 * S, rows), bf16),
            pltpu.VMEM((3, 3, channels), f32),
            pltpu.SemaphoreType.DMA((8,)),
            pltpu.VMEM((S, 2 * quarters, LANES), f32),
            pltpu.VMEM((S, 2 * quarters, LANES), f32),
            pltpu.VMEM((S, 2, quarters, LANES), f32),
            pltpu.VMEM((2, LANES + tiles * TILE, LANES), bf16),
            pltpu.VMEM((2, S, own, PER, TILE), bf16),
            pltpu.VMEM((2, tiles + SEG, PER, TILE), bf16),
            pltpu.VMEM((tiles * PER, TILE), f32),
            pltpu.VMEM((2, tiles, PER, TILE), bf16),
            pltpu.VMEM((2, S, own, PER, TILE), bf16),
            pltpu.VMEM((2, S, 2, LANES), f32),
            pltpu.VMEM((2, S, 2, LANES), f32),
            pltpu.VMEM((2, PER, channels), bf16),
            pltpu.VMEM((rows + 8, channels), f32),
            pltpu.VMEM((2, 2, rows + 8, half), f32),
            pltpu.VMEM((rows, channels), bf16),
            pltpu.VMEM((2, 2, rows, half), bf16),
            pltpu.SemaphoreType.DMA((2,)),
            pltpu.SemaphoreType.DMA((2,)),
            pltpu.SemaphoreType.DMA((2,)),
            pltpu.SemaphoreType.DMA((2,)),
            pltpu.SemaphoreType.DMA((2,)),
            pltpu.SemaphoreType.DMA((2,)),
            pltpu.SemaphoreType.DMA((2,)),
            pltpu.SemaphoreType.DMA((2,)),
            pltpu.SemaphoreType.DMA((2,)),
            pltpu.SemaphoreType.DMA((3,)),
            pltpu.SemaphoreType.DMA((3,)),
        ],
        compiler_params=pltpu.CompilerParams(
            collective_id=0, has_side_effects=True, vmem_limit_bytes=48 * 1024 * 1024
        ),
    )(*[
        pltpu.with_memory_space_constraint(value, pltpu.HBM)
        for value in (grad_out, qkv_saved.transpose(1, 0, 2), conv_saved, long_taps.T, short_taps)
    ])
    return out.transpose(1, 0, 2)


def solution(mesh):
    in_specs = (
        P("seq", "chan"),
        P("seq", None, "chan"),
        P("seq", "chan"),
        P("seq", "chan"),
        P(None, None, "chan"),
    )
    out_specs = P(("seq", "chan"), None, None)
    return jax.shard_map(
        functools.partial(on_device, mesh.shape["seq"], mesh.shape["chan"]),
        mesh=mesh, in_specs=in_specs, out_specs=out_specs, check_vma=False,
    )
```

```python
import functools
import math

import jax
import jax.numpy as jnp
from jax import lax
from jax.experimental import pallas as pl
from jax.experimental.pallas import tpu as pltpu
from jax.sharding import PartitionSpec as P

MESH = pl.DeviceIdType.MESH
f32 = jnp.float32
bf16 = jnp.bfloat16

LANES = 128
TILE = 256
PER = 16
FEW = 8
PIECES = 4
SEG = 8


def kernel(
    S, C,
    go_hbm, qkv_hbm, cv_hbm, tp_hbm, st_hbm, out_ref,
    go_ref, qkv_ref, cv_ref, tp_ref, st_ref, in_sem,
    tap_rows, tap_send, tap_recv, rev_ref, strip, x_send, x_recv, x_wide, acc, y_send, y_recv,
    edge_send, edge_recv, near_send, near_recv, eq, ez, wq, wz,
    tap_sem, x_ssem, x_rsem, y_ssem, y_rsem, e_ssem, e_rsem, h_ssem, h_rsem, o_ssem, o_rsem,
):
    rows, channels = go_ref.shape
    half = channels // 2
    piece = channels // PIECES
    tiles = S * rows // TILE
    own = rows // TILE
    part = rows // C
    me_s = lax.axis_index("seq")
    me_c = lax.axis_index("chan")

    def local(src, dst, sem):
        pltpu.make_async_copy(src, dst, sem).start()

    def landed(ref, sem):
        pltpu.make_async_copy(ref, ref, sem).wait()

    def seq_copy(src, dst, ssem, rsem, j):
        return pltpu.make_async_remote_copy(
            src_ref=src, dst_ref=dst, send_sem=ssem, recv_sem=rsem,
            device_id=(j, me_c), device_id_type=MESH,
        )

    def chan_copy(src, dst, ssem, rsem, j):
        return pltpu.make_async_remote_copy(
            src_ref=src, dst_ref=dst, send_sem=ssem, recv_sem=rsem,
            device_id=(me_s, j), device_id_type=MESH,
        )

    turn = 1 - 2 * lax.rem(me_s, 2)
    if S % 2 == 0:
        chips = S // 2
        steps = sorted(range(1, chips), key=lambda z: -min(z, chips - z))
        seq_order = [
            lax.rem(me_s // 2 + turn * z + chips, chips) * 2 + lax.rem(me_s + core, 2) for z in steps for core in range(2)
        ] + [me_s + turn]
    else:
        seq_order = [lax.rem(me_s + k, S) for k in range(1, S)]
    side = math.isqrt(C)
    if side * side == C:
        moves = sorted(
            [(x, y) for x in range(side) for y in range(side) if x + y > 0],
            key=lambda m: -(min(m[0], side - m[0]) + min(m[1], side - m[1])),
        )
        chan_order = [
            lax.rem(me_c // side + turn * x + side, side) * side + lax.rem(lax.rem(me_c, side) + turn * y + side, side)
            for x, y in moves
        ]
    else:
        chan_order = [lax.rem(me_c + k, C) for k in range(1, C)]

    barrier = pltpu.get_barrier_semaphore()

    def greet_seq(k, carry):
        pl.semaphore_signal(barrier, inc=1, device_id=(lax.rem(me_s + k, S), me_c), device_id_type=MESH)
        return carry

    def greet_chan(k, carry):
        pl.semaphore_signal(barrier, inc=1, device_id=(me_s, lax.rem(me_c + k, C)), device_id_type=MESH)
        return carry

    lax.fori_loop(1, S, greet_seq, 0)
    lax.fori_loop(1, C, greet_chan, 0)

    loads = {}

    def load(name, src, dst):
        loads[name] = pltpu.make_async_copy(src, dst, in_sem.at[len(loads)])
        loads[name].start()

    load("tp", tp_hbm, tp_ref)
    for g in range(2):
        cols = slice(g * half, (g + 1) * half)
        load(f"go{g}", go_hbm.at[:, cols], go_ref.at[:, cols])
        load(f"q{g}", qkv_hbm.at[0, :, cols], qkv_ref.at[0, :, cols])
    load("cv", cv_hbm, cv_ref)
    load("st", st_hbm, st_ref)
    load("kv", qkv_hbm.at[1:3], qkv_ref.at[1:3])

    quarters = rows // LANES
    loads["tp"].wait()
    for u in range(PIECES):
        for q in range(quarters):
            chunk = tp_ref[u * (S // 2):(u + 1) * (S // 2), q * LANES:(q + 1) * LANES].astype(f32)
            tap_rows[:, u * quarters + q, :] = chunk
    tap_send[...] = tap_rows[...].astype(bf16)

    def mix(g):
        cols = slice(g * half, (g + 1) * half)
        loads[f"go{g}"].wait()
        loads[f"q{g}"].wait()
        turned = (go_ref[:, cols].astype(f32) * qkv_ref[0, :, cols].astype(f32)).T.reshape(2, S, FEW, rows)
        paired = jnp.concatenate([turned[0], turned[1]], 1).astype(bf16)
        for h in range(own):
            x_send[g, :, h] = paired[:, :, h * TILE:(h + 1) * TILE]

    pl.semaphore_wait(barrier, S + C - 2)

    local(tap_send.at[me_s // 2], tap_recv.at[me_s], tap_sem.at[1])

    for j in seq_order:
        seq_copy(tap_send.at[j // 2], tap_recv.at[me_s], tap_sem.at[0], tap_sem.at[1], j).start()

    mix(0)

    def push_x(g):
        mine = pl.ds(me_s * own, own)
        local(x_send.at[g, me_s], x_recv.at[g, mine], x_rsem.at[g])

        for j in seq_order:
            seq_copy(x_send.at[g, j], x_recv.at[g, mine], x_ssem.at[g], x_rsem.at[g], j).start()

    push_x(0)
    mix(1)
    push_x(1)

    loads["kv"].wait()
    loads["cv"].wait()
    loads["st"].wait()
    head = slice(0, PER)
    near_send[0] = (go_ref[head].astype(f32) * cv_ref[head].astype(f32))[0:2]
    for p in range(1, 3):
        near_send[p] = qkv_ref[p, head].astype(f32)[0:2]
    near = seq_copy(near_send, near_recv, h_ssem.at[0], h_rsem.at[0], lax.rem(me_s + S - 1, S))
    near.start()

    def taps3(e, first, taps):
        return sum(taps[j:j + 1] * e[first + j:first + j + part, :] for j in range(3))

    def spread(source, dst, ssem, rsem, late):
        def block(c):
            return source(pl.ds(pl.multiple_of(c * part, part), part))

        def fits(c):
            return c >= 0 if late is None else (c == C - 1 if late else c < C - 1)

        for c in chan_order:

            @pl.when(fits(c))
            def _(c=c):
                chan_copy(block(c), dst, ssem, rsem, c).start()

        @pl.when(fits(me_c))
        def _():
            local(block(me_c), dst, rsem)

    eq[0:rows, :] = go_ref[...].astype(f32) * cv_ref[...].astype(f32)

    def query(blocks):
        for c in range(C - 1) if blocks == "first" else [C - 1]:
            wq[c * part:(c + 1) * part, :] = taps3(eq, c * part, st_ref[0]).astype(bf16)
        dst = out_ref.at[0, :, pl.ds(pl.multiple_of(me_c * channels, channels), channels)]
        spread(lambda at: wq.at[at, :], dst, o_ssem.at[PIECES], o_rsem.at[PIECES], blocks == "last")


    landed(tap_recv, tap_sem.at[1])
    down = lax.broadcasted_iota(jnp.int32, (LANES, LANES), 0)
    over = lax.broadcasted_iota(jnp.int32, (LANES, LANES), 1)
    mirror = (lax.rem(down + over, LANES) == 0).astype(f32).astype(bf16)
    rev = jnp.dot(
        tap_recv[...].reshape(S * PIECES * quarters, LANES), mirror, preferred_element_type=f32
    )
    rev_ref[...] = rev.reshape(S, PIECES, quarters, LANES)
    newer = (over == 0) | (over >= LANES - down)

    strip[:, 0:LANES, :] = jnp.zeros((PIECES, LANES, LANES), bf16)

    def build(pieces):
        def grow(s, before):
            after = []
            for u, last in zip(pieces, before):
                for q in range(quarters):
                    row = rev_ref[s, u, q:q + 1, :]
                    mixed = jnp.where(
                        newer, jnp.broadcast_to(row, (LANES, LANES)), jnp.broadcast_to(last, (LANES, LANES))
                    )
                    rolled = pltpu.roll(mixed, 0, 1, stride=1, stride_axis=0)
                    at = pl.multiple_of((s * quarters + q + 1) * LANES, LANES)
                    strip[u, pl.ds(at, LANES), :] = rolled.astype(bf16)
                    last = row
                after.append(last)
            return tuple(after)

        nothing = jnp.zeros((1, LANES), f32)
        lax.fori_loop(0, S, grow, (nothing,) * len(pieces))

    x_wide[:, tiles:tiles + SEG - 1] = jnp.zeros((2, SEG - 1, FEW, TILE), f32)

    def widen(g):
        landed(x_recv.at[g, 0:tiles], x_rsem.at[g])
        wide = x_recv[g, 0:tiles].astype(f32)
        for side_of in range(2):
            x_wide[side_of, 0:tiles] = wide[:, side_of * FEW:(side_of + 1) * FEW]

    pick = (
        lax.broadcasted_iota(jnp.int32, (8, LANES), 0) == lax.broadcasted_iota(jnp.int32, (8, LANES), 1)
    ).astype(f32).astype(bf16)

    def correlate(u):
        g, side_of = u // 2, u % 2
        for seg in range(tiles // SEG):
            n = tiles - seg * SEG
            deep = SEG * TILE
            left = jnp.concatenate(
                [x_wide[side_of, seg * SEG + d:seg * SEG + d + n].reshape(n * FEW, TILE) for d in range(SEG)], 1
            ).astype(bf16)
            right = jnp.concatenate(
                [
                    strip[u, LANES + seg * deep:LANES + (seg + 1) * deep, :],
                    strip[u, seg * deep:(seg + 1) * deep, :],
                ],
                1,
            )
            product = jnp.dot(left, right, preferred_element_type=f32)
            if seg == 0:
                acc[...] = product
            else:
                acc[0:n * FEW, :] += product
        result = acc[...].reshape(S, own * FEW, TILE).astype(bf16)
        y_send[u] = result
        local(y_send.at[u, me_s], y_recv.at[u, me_s], y_rsem.at[u])
        for j in seq_order:
            seq_copy(y_send.at[u, j], y_recv.at[u, me_s], y_ssem.at[u], y_rsem.at[u], j).start()

    def edges(g):
        heads = [
            lax.dot_general(
                pick, y_send[2 * g + a, :, :, 0:LANES].reshape(S * own * FEW, LANES), (((1,), (1,)), ((), ())),
                preferred_element_type=f32,
            )
            for a in range(2)
        ]
        second = lax.broadcasted_iota(jnp.int32, (8, LANES), 1) // FEW == lax.rem(me_s + S // 2, S)
        for j in range(S - 1):
            lane = (j + 1) * own * FEW
            base = lane // LANES * LANES
            moved = [
                pltpu.roll(
                    heads[a][:, base:base + LANES],
                    lax.rem(me_s * FEW + a * (LANES // 2) + LANES - lane % LANES, LANES), 1,
                )
                for a in range(2)
            ]
            edge_send[g, j] = jnp.where(second, moved[1], moved[0])[0:2]
        edge_send[g, S - 1] = jnp.zeros((2, LANES), f32)
        local(edge_send.at[g, me_s], edge_recv.at[g, me_s], e_rsem.at[g])
        for j in seq_order:
            seq_copy(edge_send.at[g, j], edge_recv.at[g, me_s], e_ssem.at[g], e_rsem.at[g], j).start()

    build((0, 1))
    build((2, 3))
    widen(0)
    correlate(0)
    correlate(1)
    edges(0)
    near.wait_recv()
    eq[rows:rows + 2, :] = jnp.where(me_s == S - 1, 0.0, near_recv[0])
    query("first")
    query("last")
    widen(1)
    correlate(2)
    correlate(3)
    edges(1)

    def finish(u):
        cols = slice(u * piece, (u + 1) * piece)
        landed(y_recv.at[u], y_rsem.at[u])
        wide = y_recv[u].astype(f32)
        for h in range(own):
            at = slice(h * TILE, (h + 1) * TILE)
            gz = wide[:, h * FEW:(h + 1) * FEW].reshape(piece, TILE).T
            ez[u, 0, at, :] = gz * qkv_ref[2, at, cols].astype(f32)
            ez[u, 1, at, :] = gz * qkv_ref[1, at, cols].astype(f32)
        g, a = u // 2, u % 2
        if a == 0:
            landed(edge_recv.at[g], e_rsem.at[g])
        source = lax.broadcasted_iota(jnp.int32, (2, LANES), 1) // FEW
        edge = edge_recv[g, 0]
        for k in range(1, S):
            edge = jnp.where(source == (k + a * (S // 2)) % S, edge_recv[g, k], edge)
        if a == 1:
            edge = jnp.concatenate([edge[:, LANES // 2:], edge[:, 0:LANES // 2]], 1)
        ez[u, 0, rows:rows + 2, :] = edge * near_recv[2, :, cols]
        ez[u, 1, rows:rows + 2, :] = edge * near_recv[1, :, cols]
        for c in range(C):
            for p in range(2):
                wz[u, p, c * part:(c + 1) * part, :] = taps3(
                    ez.at[u, p], c * part, st_ref[1 + p, :, cols]
                ).astype(bf16)
        dst = out_ref.at[1:3, :, pl.ds(pl.multiple_of(me_c * channels + u * piece, piece), piece)]
        spread(lambda at: wz.at[u, :, at, :], dst, o_ssem.at[u], o_rsem.at[u], None)

    for u in range(PIECES):
        finish(u)

    landed(out_ref.at[0], o_rsem.at[PIECES])
    for u in range(PIECES):
        landed(out_ref.at[1:3, :, 0:C * piece], o_rsem.at[u])

    landed(tap_recv.at[0:S - 1], tap_sem.at[0])
    landed(wq.at[0:rows - part, :], o_ssem.at[PIECES])
    near.wait_send()
    for g in range(2):
        landed(x_send.at[g, 0:S - 1], x_ssem.at[g])
        landed(edge_send.at[g, 0:S - 1], e_ssem.at[g])
    for u in range(PIECES):
        landed(y_send.at[u, 0:S - 1], y_ssem.at[u])
        landed(wz.at[u, :, 0:rows - part, :], o_ssem.at[u])


def on_device(S, C, grad_out, qkv_saved, conv_saved, long_taps, short_taps):
    rows, channels = grad_out.shape
    piece = channels // PIECES
    tiles = S * rows // TILE
    own = rows // TILE
    quarters = rows // LANES
    out = pl.pallas_call(
        functools.partial(kernel, S, C),
        out_shape=jax.ShapeDtypeStruct((3, rows // C, C * channels), bf16),
        in_specs=[pl.BlockSpec(memory_space=pltpu.HBM)] * 5,
        out_specs=pl.BlockSpec(memory_space=pl.ANY),
        scratch_shapes=[
            pltpu.VMEM((rows, channels), bf16),
            pltpu.VMEM((3, rows, channels), bf16),
            pltpu.VMEM((rows, channels), bf16),
            pltpu.VMEM((2 * S, rows), bf16),
            pltpu.VMEM((3, 3, channels), f32),
            pltpu.SemaphoreType.DMA((8,)),
            pltpu.VMEM((S // 2, PIECES * quarters, LANES), f32),
            pltpu.VMEM((S // 2, PIECES * quarters, LANES), bf16),
            pltpu.VMEM((S, PIECES * quarters, LANES), bf16),
            pltpu.VMEM((S, PIECES, quarters, LANES), f32),
            pltpu.VMEM((PIECES, LANES + tiles * TILE, LANES), bf16),
            pltpu.VMEM((2, S, own, PER, TILE), bf16),
            pltpu.VMEM((2, tiles + SEG, PER, TILE), bf16),
            pltpu.VMEM((2, tiles + SEG, FEW, TILE), f32),
            pltpu.VMEM((tiles * FEW, TILE), f32),
            pltpu.VMEM((PIECES, S, own * FEW, TILE), bf16),
            pltpu.VMEM((PIECES, S, own * FEW, TILE), bf16),
            pltpu.VMEM((2, S, 2, LANES), f32),
            pltpu.VMEM((2, S, 2, LANES), f32),
            pltpu.VMEM((3, 2, channels), f32),
            pltpu.VMEM((3, 2, channels), f32),
            pltpu.VMEM((rows + 8, channels), f32),
            pltpu.VMEM((PIECES, 2, rows + 8, piece), f32),
            pltpu.VMEM((rows, channels), bf16),
            pltpu.VMEM((PIECES, 2, rows, piece), bf16),
            pltpu.SemaphoreType.DMA((2,)),
            pltpu.SemaphoreType.DMA((2,)),
            pltpu.SemaphoreType.DMA((2,)),
            pltpu.SemaphoreType.DMA((PIECES,)),
            pltpu.SemaphoreType.DMA((PIECES,)),
            pltpu.SemaphoreType.DMA((PIECES,)),
            pltpu.SemaphoreType.DMA((PIECES,)),
            pltpu.SemaphoreType.DMA((2,)),
            pltpu.SemaphoreType.DMA((2,)),
            pltpu.SemaphoreType.DMA((PIECES + 1,)),
            pltpu.SemaphoreType.DMA((PIECES + 1,)),
        ],
        compiler_params=pltpu.CompilerParams(
            collective_id=0, has_side_effects=True, vmem_limit_bytes=48 * 1024 * 1024
        ),
    )(*[
        pltpu.with_memory_space_constraint(value, pltpu.HBM)
        for value in (grad_out, qkv_saved.transpose(1, 0, 2), conv_saved, long_taps.T, short_taps)
    ])
    return out.transpose(1, 0, 2)


def solution(mesh):
    in_specs = (
        P("seq", "chan"),
        P("seq", None, "chan"),
        P("seq", "chan"),
        P("seq", "chan"),
        P(None, None, "chan"),
    )
    out_specs = P(("seq", "chan"), None, None)
    return jax.shard_map(
        functools.partial(on_device, mesh.shape["seq"], mesh.shape["chan"]),
        mesh=mesh, in_specs=in_specs, out_specs=out_specs, check_vma=False,
    )
```

```python
import functools
import math

import jax
import jax.numpy as jnp
from jax import lax
from jax.experimental import pallas as pl
from jax.experimental.pallas import tpu as pltpu
from jax.sharding import PartitionSpec as P

MESH = pl.DeviceIdType.MESH
f32 = jnp.float32
bf16 = jnp.bfloat16

LANES = 128
TILE = 256
PER = 16
FEW = 8
PIECES = 4
SEG = 8


def kernel(
    S, C,
    go_hbm, qkv_hbm, cv_hbm, tp_hbm, st_hbm, out_ref,
    go_ref, qkv_ref, cv_ref, tp_ref, st_ref, in_sem,
    tap_rows, tap_send, tap_recv, rev_ref, strip, x_send, x_recv, x_wide, acc, y_send, y_recv,
    edge_send, edge_recv, near_send, near_recv, eq, ez, wq, wz,
    tap_sem, x_ssem, x_rsem, y_ssem, y_rsem, e_ssem, e_rsem, h_ssem, h_rsem, o_ssem, o_rsem,
):
    rows, channels = go_ref.shape
    half = channels // 2
    piece = channels // PIECES
    tiles = S * rows // TILE
    own = rows // TILE
    part = rows // C
    me_s = lax.axis_index("seq")
    me_c = lax.axis_index("chan")

    def local(src, dst, sem):
        pltpu.make_async_copy(src, dst, sem).start()

    def landed(ref, sem):
        pltpu.make_async_copy(ref, ref, sem).wait()

    def seq_copy(src, dst, ssem, rsem, j):
        return pltpu.make_async_remote_copy(
            src_ref=src, dst_ref=dst, send_sem=ssem, recv_sem=rsem,
            device_id=(j, me_c), device_id_type=MESH,
        )

    def chan_copy(src, dst, ssem, rsem, j):
        return pltpu.make_async_remote_copy(
            src_ref=src, dst_ref=dst, send_sem=ssem, recv_sem=rsem,
            device_id=(me_s, j), device_id_type=MESH,
        )

    turn = 1 - 2 * lax.rem(me_s, 2)
    steps = sorted(range(1, S), key=lambda k: -min(k, S - k))
    seq_order = [lax.rem(me_s + k, S) for k in steps]
    side = math.isqrt(C)
    if side * side == C:
        moves = sorted(
            [(x, y) for x in range(side) for y in range(side) if x + y > 0],
            key=lambda m: -(min(m[0], side - m[0]) + min(m[1], side - m[1])),
        )
        chan_order = [
            lax.rem(me_c // side + turn * x + side, side) * side + lax.rem(lax.rem(me_c, side) + turn * y + side, side)
            for x, y in moves
        ]
    else:
        chan_order = [lax.rem(me_c + k, C) for k in range(1, C)]

    barrier = pltpu.get_barrier_semaphore()

    def greet_seq(k, carry):
        pl.semaphore_signal(barrier, inc=1, device_id=(lax.rem(me_s + k, S), me_c), device_id_type=MESH)
        return carry

    def greet_chan(k, carry):
        pl.semaphore_signal(barrier, inc=1, device_id=(me_s, lax.rem(me_c + k, C)), device_id_type=MESH)
        return carry

    lax.fori_loop(1, S, greet_seq, 0)
    lax.fori_loop(1, C, greet_chan, 0)

    loads = {}

    def load(name, src, dst):
        loads[name] = pltpu.make_async_copy(src, dst, in_sem.at[len(loads)])
        loads[name].start()

    load("tp", tp_hbm, tp_ref)
    for g in range(2):
        cols = slice(g * half, (g + 1) * half)
        load(f"go{g}", go_hbm.at[:, cols], go_ref.at[:, cols])
        load(f"q{g}", qkv_hbm.at[0, :, cols], qkv_ref.at[0, :, cols])
    load("cv", cv_hbm, cv_ref)
    load("st", st_hbm, st_ref)
    load("kv", qkv_hbm.at[1:3], qkv_ref.at[1:3])

    quarters = rows // LANES
    loads["tp"].wait()
    for u in range(PIECES):
        for q in range(quarters):
            chunk = tp_ref[u * (S // 2):(u + 1) * (S // 2), q * LANES:(q + 1) * LANES].astype(f32)
            tap_rows[:, u * quarters + q, :] = chunk
    tap_send[...] = tap_rows[...].astype(bf16)

    def mix(g):
        cols = slice(g * half, (g + 1) * half)
        loads[f"go{g}"].wait()
        loads[f"q{g}"].wait()
        turned = (go_ref[:, cols].astype(f32) * qkv_ref[0, :, cols].astype(f32)).T.reshape(2, S, FEW, rows)
        paired = jnp.concatenate([turned[0], turned[1]], 1).astype(bf16)
        for h in range(own):
            x_send[g, :, h] = paired[:, :, h * TILE:(h + 1) * TILE]

    pl.semaphore_wait(barrier, S + C - 2)

    local(tap_send.at[me_s // 2], tap_recv.at[me_s], tap_sem.at[1])

    for j in seq_order:
        seq_copy(tap_send.at[j // 2], tap_recv.at[me_s], tap_sem.at[0], tap_sem.at[1], j).start()

    mix(0)

    def push_x(g):
        mine = pl.ds(me_s * own, own)
        local(x_send.at[g, me_s], x_recv.at[g, mine], x_rsem.at[g])

        for j in seq_order:
            seq_copy(x_send.at[g, j], x_recv.at[g, mine], x_ssem.at[g], x_rsem.at[g], j).start()

    push_x(0)
    mix(1)
    push_x(1)

    loads["kv"].wait()
    loads["cv"].wait()
    loads["st"].wait()
    head = slice(0, PER)
    near_send[0] = (go_ref[head].astype(f32) * cv_ref[head].astype(f32))[0:2]
    for p in range(1, 3):
        near_send[p] = qkv_ref[p, head].astype(f32)[0:2]
    near = seq_copy(near_send, near_recv, h_ssem.at[0], h_rsem.at[0], lax.rem(me_s + S - 1, S))
    near.start()

    def taps3(e, first, taps):
        return sum(taps[j:j + 1] * e[first + j:first + j + part, :] for j in range(3))

    def spread(source, dst, ssem, rsem, late):
        def block(c):
            return source(pl.ds(pl.multiple_of(c * part, part), part))

        def fits(c):
            return c >= 0 if late is None else (c == C - 1 if late else c < C - 1)

        for c in chan_order:

            @pl.when(fits(c))
            def _(c=c):
                chan_copy(block(c), dst, ssem, rsem, c).start()

        @pl.when(fits(me_c))
        def _():
            local(block(me_c), dst, rsem)

    eq[0:rows, :] = go_ref[...].astype(f32) * cv_ref[...].astype(f32)

    def query(blocks):
        for c in range(C - 1) if blocks == "first" else [C - 1]:
            wq[c * part:(c + 1) * part, :] = taps3(eq, c * part, st_ref[0]).astype(bf16)
        dst = out_ref.at[0, :, pl.ds(pl.multiple_of(me_c * channels, channels), channels)]
        spread(lambda at: wq.at[at, :], dst, o_ssem.at[PIECES], o_rsem.at[PIECES], blocks == "last")


    landed(tap_recv, tap_sem.at[1])
    down = lax.broadcasted_iota(jnp.int32, (LANES, LANES), 0)
    over = lax.broadcasted_iota(jnp.int32, (LANES, LANES), 1)
    mirror = (lax.rem(down + over, LANES) == 0).astype(f32).astype(bf16)
    rev = jnp.dot(
        tap_recv[...].reshape(S * PIECES * quarters, LANES), mirror, preferred_element_type=f32
    )
    rev_ref[...] = rev.reshape(S, PIECES, quarters, LANES)
    newer = (over == 0) | (over >= LANES - down)

    strip[:, 0:LANES, :] = jnp.zeros((PIECES, LANES, LANES), bf16)

    def build(pieces):
        def grow(s, before):
            after = []
            for u, last in zip(pieces, before):
                for q in range(quarters):
                    row = rev_ref[s, u, q:q + 1, :]
                    mixed = jnp.where(
                        newer, jnp.broadcast_to(row, (LANES, LANES)), jnp.broadcast_to(last, (LANES, LANES))
                    )
                    rolled = pltpu.roll(mixed, 0, 1, stride=1, stride_axis=0)
                    at = pl.multiple_of((s * quarters + q + 1) * LANES, LANES)
                    strip[u, pl.ds(at, LANES), :] = rolled.astype(bf16)
                    last = row
                after.append(last)
            return tuple(after)

        nothing = jnp.zeros((1, LANES), f32)
        lax.fori_loop(0, S, grow, (nothing,) * len(pieces))

    x_wide[:, tiles:tiles + SEG - 1] = jnp.zeros((2, SEG - 1, FEW, TILE), f32)

    def widen(g):
        landed(x_recv.at[g, 0:tiles], x_rsem.at[g])
        wide = x_recv[g, 0:tiles].astype(f32)
        for side_of in range(2):
            x_wide[side_of, 0:tiles] = wide[:, side_of * FEW:(side_of + 1) * FEW]

    pick = (
        lax.broadcasted_iota(jnp.int32, (8, LANES), 0) == lax.broadcasted_iota(jnp.int32, (8, LANES), 1)
    ).astype(f32).astype(bf16)

    def correlate(u):
        g, side_of = u // 2, u % 2
        for seg in range(tiles // SEG):
            n = tiles - seg * SEG
            deep = SEG * TILE
            left = jnp.concatenate(
                [x_wide[side_of, seg * SEG + d:seg * SEG + d + n].reshape(n * FEW, TILE) for d in range(SEG)], 1
            ).astype(bf16)
            right = jnp.concatenate(
                [
                    strip[u, LANES + seg * deep:LANES + (seg + 1) * deep, :],
                    strip[u, seg * deep:(seg + 1) * deep, :],
                ],
                1,
            )
            product = jnp.dot(left, right, preferred_element_type=f32)
            if seg == 0:
                acc[...] = product
            else:
                acc[0:n * FEW, :] += product
        result = acc[...].reshape(S, own * FEW, TILE).astype(bf16)
        y_send[u] = result
        local(y_send.at[u, me_s], y_recv.at[u, me_s], y_rsem.at[u])
        for j in seq_order:
            seq_copy(y_send.at[u, j], y_recv.at[u, me_s], y_ssem.at[u], y_rsem.at[u], j).start()

    def edges(g):
        heads = [
            lax.dot_general(
                pick, y_send[2 * g + a, :, :, 0:LANES].reshape(S * own * FEW, LANES), (((1,), (1,)), ((), ())),
                preferred_element_type=f32,
            )
            for a in range(2)
        ]
        second = lax.broadcasted_iota(jnp.int32, (8, LANES), 1) // FEW == lax.rem(me_s + S // 2, S)
        for j in range(S - 1):
            lane = (j + 1) * own * FEW
            base = lane // LANES * LANES
            moved = [
                pltpu.roll(
                    heads[a][:, base:base + LANES],
                    lax.rem(me_s * FEW + a * (LANES // 2) + LANES - lane % LANES, LANES), 1,
                )
                for a in range(2)
            ]
            edge_send[g, j] = jnp.where(second, moved[1], moved[0])[0:2]
        edge_send[g, S - 1] = jnp.zeros((2, LANES), f32)
        local(edge_send.at[g, me_s], edge_recv.at[g, me_s], e_rsem.at[g])
        for j in seq_order:
            seq_copy(edge_send.at[g, j], edge_recv.at[g, me_s], e_ssem.at[g], e_rsem.at[g], j).start()

    build((0, 1))
    build((2, 3))
    widen(0)
    correlate(0)
    correlate(1)
    edges(0)
    near.wait_recv()
    eq[rows:rows + 2, :] = jnp.where(me_s == S - 1, 0.0, near_recv[0])
    query("first")
    query("last")
    widen(1)
    correlate(2)
    correlate(3)
    edges(1)

    def finish(u):
        cols = slice(u * piece, (u + 1) * piece)
        landed(y_recv.at[u], y_rsem.at[u])
        wide = y_recv[u].astype(f32)
        for h in range(own):
            at = slice(h * TILE, (h + 1) * TILE)
            gz = wide[:, h * FEW:(h + 1) * FEW].reshape(piece, TILE).T
            ez[u, 0, at, :] = gz * qkv_ref[2, at, cols].astype(f32)
            ez[u, 1, at, :] = gz * qkv_ref[1, at, cols].astype(f32)
        g, a = u // 2, u % 2
        if a == 0:
            landed(edge_recv.at[g], e_rsem.at[g])
        source = lax.broadcasted_iota(jnp.int32, (2, LANES), 1) // FEW
        edge = edge_recv[g, 0]
        for k in range(1, S):
            edge = jnp.where(source == (k + a * (S // 2)) % S, edge_recv[g, k], edge)
        if a == 1:
            edge = jnp.concatenate([edge[:, LANES // 2:], edge[:, 0:LANES // 2]], 1)
        ez[u, 0, rows:rows + 2, :] = edge * near_recv[2, :, cols]
        ez[u, 1, rows:rows + 2, :] = edge * near_recv[1, :, cols]
        for c in range(C):
            for p in range(2):
                wz[u, p, c * part:(c + 1) * part, :] = taps3(
                    ez.at[u, p], c * part, st_ref[1 + p, :, cols]
                ).astype(bf16)
        dst = out_ref.at[1:3, :, pl.ds(pl.multiple_of(me_c * channels + u * piece, piece), piece)]
        spread(lambda at: wz.at[u, :, at, :], dst, o_ssem.at[u], o_rsem.at[u], None)

    for u in range(PIECES):
        finish(u)

    landed(out_ref.at[0], o_rsem.at[PIECES])
    for u in range(PIECES):
        landed(out_ref.at[1:3, :, 0:C * piece], o_rsem.at[u])

    landed(tap_recv.at[0:S - 1], tap_sem.at[0])
    landed(wq.at[0:rows - part, :], o_ssem.at[PIECES])
    near.wait_send()
    for g in range(2):
        landed(x_send.at[g, 0:S - 1], x_ssem.at[g])
        landed(edge_send.at[g, 0:S - 1], e_ssem.at[g])
    for u in range(PIECES):
        landed(y_send.at[u, 0:S - 1], y_ssem.at[u])
        landed(wz.at[u, :, 0:rows - part, :], o_ssem.at[u])


def on_device(S, C, grad_out, qkv_saved, conv_saved, long_taps, short_taps):
    rows, channels = grad_out.shape
    piece = channels // PIECES
    tiles = S * rows // TILE
    own = rows // TILE
    quarters = rows // LANES
    out = pl.pallas_call(
        functools.partial(kernel, S, C),
        out_shape=jax.ShapeDtypeStruct((3, rows // C, C * channels), bf16),
        in_specs=[pl.BlockSpec(memory_space=pltpu.HBM)] * 5,
        out_specs=pl.BlockSpec(memory_space=pl.ANY),
        scratch_shapes=[
            pltpu.VMEM((rows, channels), bf16),
            pltpu.VMEM((3, rows, channels), bf16),
            pltpu.VMEM((rows, channels), bf16),
            pltpu.VMEM((2 * S, rows), bf16),
            pltpu.VMEM((3, 3, channels), f32),
            pltpu.SemaphoreType.DMA((8,)),
            pltpu.VMEM((S // 2, PIECES * quarters, LANES), f32),
            pltpu.VMEM((S // 2, PIECES * quarters, LANES), bf16),
            pltpu.VMEM((S, PIECES * quarters, LANES), bf16),
            pltpu.VMEM((S, PIECES, quarters, LANES), f32),
            pltpu.VMEM((PIECES, LANES + tiles * TILE, LANES), bf16),
            pltpu.VMEM((2, S, own, PER, TILE), bf16),
            pltpu.VMEM((2, tiles + SEG, PER, TILE), bf16),
            pltpu.VMEM((2, tiles + SEG, FEW, TILE), f32),
            pltpu.VMEM((tiles * FEW, TILE), f32),
            pltpu.VMEM((PIECES, S, own * FEW, TILE), bf16),
            pltpu.VMEM((PIECES, S, own * FEW, TILE), bf16),
            pltpu.VMEM((2, S, 2, LANES), f32),
            pltpu.VMEM((2, S, 2, LANES), f32),
            pltpu.VMEM((3, 2, channels), f32),
            pltpu.VMEM((3, 2, channels), f32),
            pltpu.VMEM((rows + 8, channels), f32),
            pltpu.VMEM((PIECES, 2, rows + 8, piece), f32),
            pltpu.VMEM((rows, channels), bf16),
            pltpu.VMEM((PIECES, 2, rows, piece), bf16),
            pltpu.SemaphoreType.DMA((2,)),
            pltpu.SemaphoreType.DMA((2,)),
            pltpu.SemaphoreType.DMA((2,)),
            pltpu.SemaphoreType.DMA((PIECES,)),
            pltpu.SemaphoreType.DMA((PIECES,)),
            pltpu.SemaphoreType.DMA((PIECES,)),
            pltpu.SemaphoreType.DMA((PIECES,)),
            pltpu.SemaphoreType.DMA((2,)),
            pltpu.SemaphoreType.DMA((2,)),
            pltpu.SemaphoreType.DMA((PIECES + 1,)),
            pltpu.SemaphoreType.DMA((PIECES + 1,)),
        ],
        compiler_params=pltpu.CompilerParams(
            collective_id=0, has_side_effects=True, vmem_limit_bytes=48 * 1024 * 1024
        ),
    )(*[
        pltpu.with_memory_space_constraint(value, pltpu.HBM)
        for value in (grad_out, qkv_saved.transpose(1, 0, 2), conv_saved, long_taps.T, short_taps)
    ])
    return out.transpose(1, 0, 2)


def solution(mesh):
    in_specs = (
        P("seq", "chan"),
        P("seq", None, "chan"),
        P("seq", "chan"),
        P("seq", "chan"),
        P(None, None, "chan"),
    )
    out_specs = P(("seq", "chan"), None, None)
    return jax.shard_map(
        functools.partial(on_device, mesh.shape["seq"], mesh.shape["chan"]),
        mesh=mesh, in_specs=in_specs, out_specs=out_specs, check_vma=False,
    )
```
